512 devices in a mesh: tok: 32 (over y, z_lo), col: 16 (over x, z_hi, core).
Axes of the slice: x: 4, y: 8, z: 8 (z_hi: 2, z_lo: 4; z = z_hi * 4 + z_lo), core: 2. Of those that a mesh axis runs over, the one named last changes fastest.
Arguments:
- grads: bfloat16 [2048, 27648], P('tok', 'col'), may hold values from -6 to 6
- acts: bfloat16 [2048, 5120], P('col', 'tok'), may hold values from -6 to 6
- grad_basis: bfloat16 [27648, 13824], P('col', 'tok'), may hold values from -0.0625 to 0.0625
- act_basis: bfloat16 [5120, 5120], P('tok', 'col'), may hold values from -0.15625 to 0.15625
Outputs:
- corrected_diag: float32 [13824, 5120], P('tok', 'col')
The draws below stay inside these ranges and needn't reach their ends.
All inputs are finite; a program needn't handle non-finite values.
Results may differ from the reference program's by a relative error of at most 0.0027.
Values may be sent and summed in bfloat16 or wider, within the bound.
No kernel may reach another device: no remote copies, remote signals or barrier semaphores. Data moves between devices by JAX's collectives and lax.ppermute only.
A program may use at most 64 MiB of HBM per device.

```python
import jax
import jax.numpy as jnp

IN = 5120
OUT = 27648
OUTW = 13824
TOKENS = 2048


def strengthened(array, stream_key, source, target, blocks, factor):
    owner, partner = [(jnp.arange(array.shape[dim]) // (array.shape[dim] // blocks)).reshape([-1 if axis == dim else 1 for axis in range(array.ndim)]) for dim in (source, target)]
    chosen = jax.random.permutation(stream_key, blocks)[partner]
    strong = (owner == chosen) | (owner == (partner + blocks // 2) % blocks)
    return jnp.where(strong, factor * array, array)


def level_of(stream_key, dims, pieces, low, top_value):
    gain = 1.0
    for dim, shards_of in pieces:
        heights = jax.random.uniform(jax.random.fold_in(jax.random.fold_in(stream_key, 6), dim), (shards_of,), jnp.float32, low / len(pieces), top_value / len(pieces))
        gain = gain * jnp.repeat(jnp.exp(heights), dims[dim] // shards_of).reshape((-1,) + (1,) * (len(dims) - 1 - dim))
    return gain


def gaussian(own_key, dims, deviation, most, split=(), held_as=jnp.bfloat16):
    loudness = level_of(own_key, dims, split, -0.22, 0.18) if split else 1.0
    entries = jax.random.normal(own_key, dims, jnp.float32) * deviation * loudness
    return jnp.minimum(jnp.maximum(entries, -most), most).astype(held_as)


def heavy_noise(own_key, shape, scale, bound, shards, heavy, dtype=jnp.bfloat16):
    values = scale * jax.random.normal(own_key, shape, jnp.float32)
    if shards:
        values = values * level_of(own_key, shape, shards, -0.22, 0.18)
    return jnp.clip(strengthened(values, jax.random.fold_in(own_key, 3), *heavy), -bound, bound).astype(dtype)


def setup_inputs(seed: int = 0) -> dict:
    seeds = jax.random.split(jax.random.key(seed), 5)
    return {
        "grads": gaussian(seeds[0], (TOKENS, OUT), 1.0, 6.0, ((0, 32), (1, 16))),
        "acts": gaussian(seeds[1], (TOKENS, IN), 1.0, 6.0, ((0, 16), (1, 32))),
        "grad_basis": heavy_noise(seeds[2], (OUT, OUTW), OUT ** -0.5, 0.0625, ((0, 16), (1, 32)), (0, 1, 32, 2.75)),
        "act_basis": heavy_noise(seeds[3], (IN, IN), IN ** -0.5, 0.15625, ((0, 32), (1, 16)), (0, 1, 32, 2.75)),
    }


def reference(grads, acts, grad_basis, act_basis):
    rot_grad = jnp.dot(grads, grad_basis, preferred_element_type=jnp.float32)
    sq_grad = (rot_grad * rot_grad).astype(jnp.bfloat16)
    rot_act = jnp.dot(acts, act_basis, preferred_element_type=jnp.float32)
    sq_act = (rot_act * rot_act).astype(jnp.bfloat16)
    total = jnp.dot(sq_grad.T, sq_act, preferred_element_type=jnp.float32)
    return total / jnp.float32(TOKENS)
```

```python
import jax
import jax.numpy as jnp
from jax import lax
from jax.sharding import Mesh, PartitionSpec as P

F32, BF16 = jnp.float32, jnp.bfloat16
SPLIT = (8, 4, 4, 2, 2)
AXES = ("y", "zl", "x", "zh", "core")
TOK, COL = ("y", "zl"), ("x", "zh", "core")


def dot(a, b):
    return jnp.dot(a, b, preferred_element_type=F32)


def shift(value, axis, by):
    n = lax.axis_size(axis)
    return lax.ppermute(value, axis, [(i, (i + by) % n) for i in range(n)])


def swap(value, axis, bit):
    return lax.ppermute(value, axis, [(i, i ^ bit) for i in range(lax.axis_size(axis))])


def ordered(first, mine, other):
    return jnp.stack([jnp.where(first, mine, other), jnp.where(first, other, mine)])


def squared_acts(acts, act_basis):
    rows, feats = acts.shape
    basis = lax.all_gather(act_basis, "zl", axis=0)
    part = lax.all_to_all(acts.reshape(4, rows // 4, feats), "zl", 0, 0)
    core, zh = lax.axis_index("core"), lax.axis_index("zh")
    part = ordered(zh == 0, part, swap(part, "zh", 1))
    part = lax.all_gather(part, "x", axis=0)
    part = ordered(core == 0, part, swap(part, "core", 1))
    part = part.reshape(16, 4, rows // 4, feats)
    rot = sum(dot(part[:, s].reshape(-1, feats), basis[s]) for s in range(4))
    cols = rot.shape[-1]
    rot = rot.astype(BF16).reshape(2, 8, rows // 4, cols).transpose(1, 0, 2, 3)
    rot = lax.all_to_all(rot, "y", 0, 0).astype(F32).sum(0)
    sq = lax.all_gather((rot * rot).astype(BF16), "zl", axis=0)
    sq = sq.transpose(1, 0, 2, 3).reshape(-1, cols)
    return lax.all_gather(sq, "y", axis=0, tiled=True)


def squared_grads(blocks, own_basis, other_basis):
    rows = jnp.concatenate(blocks, 0)
    part = jnp.stack([dot(rows, b).astype(BF16).reshape(8, rows.shape[0] // 8, -1) for b in (own_basis, other_basis)], 1)
    part = lax.all_to_all(part, ("core", "x"), 0, 0).astype(F32).sum(0)
    rot = part + swap(part.astype(BF16), "zh", 1).astype(F32)
    sq = (rot * rot).astype(BF16)
    sq = ordered(lax.axis_index("zl") % 2 == 0, sq[0], swap(sq[1], "zl", 1))
    sq = lax.all_gather(sq, "x", axis=0)
    sq = ordered(lax.axis_index("core") == 0, sq, swap(sq, "core", 1))
    return sq.reshape(-1, sq.shape[-1])


def on_device(grads, acts, grad_basis, act_basis):
    half = grads.shape[0]
    block = ordered(lax.axis_index("zl") < 2, grads, swap(grads, "zl", 2)).reshape(2 * half, -1)
    other_basis = swap(grad_basis, "zl", 1)
    right, left = [block], [block]
    for _ in range(3):
        right.append(shift(right[-1], "y", 1))
        left.append(shift(left[-1], "y", -1))
    last = jnp.concatenate([shift(right[3][:half], "y", 1), shift(left[3][half:], "y", -1)], 0)
    sq_act = squared_acts(acts, act_basis)
    near = squared_grads([right[1], block, left[1], left[2]], grad_basis, other_basis)
    far = squared_grads([left[3], last, right[3], right[2]], grad_basis, other_basis)
    tokens = sq_act.shape[0]
    at = (lax.axis_index("y") + 7) % 8 * (tokens // 8)
    sq_act = lax.dynamic_slice_in_dim(jnp.concatenate([sq_act, sq_act], 0), at, tokens, 0)
    total = sum(
        lax.dot_general(g, a, (((0,), (0,)), ((), ())), preferred_element_type=F32)
        for g, a in ((near, sq_act[: tokens // 2]), (far, sq_act[tokens // 2 :]))
    )
    return total / F32(tokens)


def solution(mesh):
    return jax.shard_map(
        on_device,
        mesh=Mesh(mesh.devices.reshape(SPLIT), AXES),
        in_specs=(P(TOK, COL), P(COL, TOK), P(COL, TOK), P(TOK, COL)),
        out_specs=P(TOK, COL),
        check_vma=False,
    )
```

```python
import jax
import jax.numpy as jnp
from jax import lax
from jax.experimental import pallas as pl
from jax.experimental.pallas import tpu as pltpu
from jax.sharding import Mesh, PartitionSpec as P

F32, BF16 = jnp.float32, jnp.bfloat16
SPLIT = (8, 2, 2, 4, 2, 2)
AXES = ("y", "zq", "zp", "x", "zh", "core")
TOK, COL = ("y", "zq", "zp"), ("x", "zh", "core")


def dot(a, b):
    return jnp.dot(a, b, preferred_element_type=F32)


def tie(values, earlier=()):
    n = len(values)
    whole = pl.BlockSpec(memory_space=pl.ANY)
    return pl.pallas_call(
        lambda *refs: None,
        out_shape=[jax.ShapeDtypeStruct(v.shape, v.dtype) for v in values],
        in_specs=[whole] * (n + len(earlier)),
        out_specs=[whole] * n,
        input_output_aliases={i: i for i in range(n)},
    )(*values, *earlier)


def shift(value, axis, by):
    n = lax.axis_size(axis)
    return lax.ppermute(value, axis, [(i, (i + by) % n) for i in range(n)])


def swap(value, axis):
    return lax.ppermute(value, axis, [(0, 1), (1, 0)])


def ordered(axis, mine, other):
    first = lax.axis_index(axis) == 0
    return jnp.stack([jnp.where(first, mine, other), jnp.where(first, other, mine)])


def spread(value, axis):
    parts = [value] + [lax.ppermute(value, axis, [(i, i ^ k) for i in range(4)]) for k in (1, 2, 3)]
    me = lax.axis_index(axis)
    odd, high = me % 2 == 1, me >= 2
    parts = [jnp.where(odd, parts[s ^ 1], parts[s]) for s in range(4)]
    return jnp.stack([jnp.where(high, parts[s ^ 2], parts[s]) for s in range(4)])


def partial_kernel(zp_ref, all_ref, own_ref, low_ref, high_ref, out_ref, rows, bases, outs, sems):
    n, low = rows.shape[1], low_ref.shape[0]
    loads = [
        (own_ref, bases.at[0]),
        (all_ref.at[pl.ds(0, n)], rows.at[0]),
        (low_ref, bases.at[1, pl.ds(0, low)]),
        (high_ref, bases.at[1, pl.ds(low, high_ref.shape[0])]),
        (all_ref.at[pl.ds(n, n)], rows.at[1]),
    ]
    loads = [pltpu.make_async_copy(a, b, sems.at[i]) for i, (a, b) in enumerate(loads)]
    for load in loads:
        load.start()
    zp = zp_ref[0]
    stores = []
    for h, which, needed in ((0, 0, loads[:2]), (0, 1, loads[2:4]), (1, 0, loads[4:]), (1, 1, ())):
        for load in needed:
            load.wait()
        part = lax.dot_general(
            bases[which], rows[h], (((1,), (1,)), ((), ())), preferred_element_type=F32
        ).astype(BF16)
        at, width = len(stores), outs.shape[3]
        for i in range(4):
            outs[at, i] = part[:, i * width : (i + 1) * width]
        place = zp if which == 0 else 1 - zp
        stores.append(
            pltpu.make_async_copy(outs.at[at], out_ref.at[pl.ds(place * 8 + h * 4, 4)], sems.at[5 + at])
        )
        stores[-1].start()
    for store in stores:
        store.wait()


def partial_sums(gathered, own, other):
    rows, feats = gathered.shape[0] // 2, gathered.shape[1]
    outs = own.shape[0]
    whole = pl.BlockSpec(memory_space=pl.ANY)
    return pl.pallas_call(
        partial_kernel,
        out_shape=jax.ShapeDtypeStruct((16, outs, rows // 4), BF16),
        in_specs=[pl.BlockSpec(memory_space=pltpu.SMEM)] + [whole] * 4,
        out_specs=whole,
        scratch_shapes=[
            pltpu.VMEM((2, rows, feats), BF16),
            pltpu.VMEM((2, outs, feats), BF16),
            pltpu.VMEM((4, 4, outs, rows // 4), BF16),
            pltpu.SemaphoreType.DMA((9,)),
        ],
        compiler_params=pltpu.CompilerParams(vmem_limit_bytes=60 * 2**20),
        cost_estimate=pl.CostEstimate(
            flops=8 * rows * feats * outs, bytes_accessed=4 * rows * feats, transcendentals=0
        ),
    )(lax.axis_index("zp").reshape(1), gathered, own, *other)


def on_device(grads, acts, grad_basis, act_basis):
    half = grads.shape[0]
    quarter, feats = acts.shape[0] // 4, acts.shape[1]
    cols = act_basis.shape[1]
    own_basis = grad_basis.T

    other = swap(grads, "zq")
    act = lax.all_to_all(acts.reshape(4, quarter, feats), ("zq", "zp"), 0, 0)
    other, act = tie([other, act])
    gathered = lax.all_gather(jnp.concatenate([grads, other], 0), "y", axis=0, tiled=True)

    act = ordered("zh", act, swap(act, "zh"))
    cut = 256
    send, act, act_basis = tie([own_basis[:cut], act, act_basis])
    other_basis = [swap(send, "zp")]
    basis = spread(act_basis, ("zq", "zp"))
    act = spread(act, "x")
    send, act = tie([own_basis[cut:], act], other_basis)
    other_basis.append(swap(send, "zp"))
    act = ordered("core", act, swap(act, "core"))
    act = act.reshape(16, 4, quarter, feats)
    rot = sum(dot(act[:, s].reshape(-1, feats), basis[s]) for s in range(4))
    rot = rot.astype(BF16).reshape(2, 8, quarter, cols).transpose(1, 0, 2, 3)
    rot = lax.all_to_all(rot, "y", 0, 0)
    (rot,) = tie([rot], other_basis)
    rot = rot.astype(F32).sum(0)
    sq = spread((rot * rot).astype(BF16), ("zq", "zp"))
    sq = sq.reshape(2, 2, 2, quarter, cols)
    first = lax.axis_index("zq") == 0
    sq = jnp.stack([jnp.where(first, sq[:, :, 0], sq[:, :, 1]), jnp.where(first, sq[:, :, 1], sq[:, :, 0])], 1)
    sq = sq.reshape(-1, cols)
    sq_act = lax.all_gather(sq, "y", axis=0, tiled=True)

    part = partial_sums(gathered, own_basis, other_basis)
    part = lax.all_to_all(part, ("zp", "core", "x"), 0, 0)
    part = part.transpose(0, 2, 1).reshape(2, 8, 2 * half, -1).astype(F32).sum(1)
    rot = part + swap(part.astype(BF16), "zh").astype(F32)
    sq = lax.all_gather((rot * rot).astype(BF16), "x", axis=0)
    mine, there = (v.reshape(-1, v.shape[-1]) for v in (sq, swap(sq, "core")))
    tokens = sq_act.shape[0] // 2
    core = lax.axis_index("core")
    total = sum(
        lax.dot_general(
            g,
            lax.dynamic_slice_in_dim(sq_act, at * tokens, tokens, 0),
            (((0,), (0,)), ((), ())),
            preferred_element_type=F32,
        )
        for g, at in ((mine, core), (there, 1 - core))
    )
    return total / F32(2 * tokens)


def solution(mesh):
    return jax.shard_map(
        on_device,
        mesh=Mesh(mesh.devices.reshape(SPLIT), AXES),
        in_specs=(P(TOK, COL), P(COL, TOK), P(COL, TOK), P(TOK, COL)),
        out_specs=P(TOK, COL),
        check_vma=False,
    )
```

```python
import jax
import jax.numpy as jnp
from jax import lax
from jax.experimental import pallas as pl
from jax.experimental.pallas import tpu as pltpu
from jax.sharding import Mesh, PartitionSpec as P

F32, BF16 = jnp.float32, jnp.bfloat16
SPLIT = (8, 2, 2, 4, 2, 2)
AXES = ("y", "zq", "zp", "x", "zh", "core")
TOK, COL = ("y", "zq", "zp"), ("x", "zh", "core")


def dot(a, b):
    return jnp.dot(a, b, preferred_element_type=F32)


def tie(values, earlier=()):
    n = len(values)
    whole = pl.BlockSpec(memory_space=pl.ANY)
    return pl.pallas_call(
        lambda *refs: None,
        out_shape=[jax.ShapeDtypeStruct(v.shape, v.dtype) for v in values],
        in_specs=[whole] * (n + len(earlier)),
        out_specs=[whole] * n,
        input_output_aliases={i: i for i in range(n)},
    )(*values, *earlier)


def shift(value, axis, by):
    n = lax.axis_size(axis)
    return lax.ppermute(value, axis, [(i, (i + by) % n) for i in range(n)])


def swap(value, axis):
    return lax.ppermute(value, axis, [(0, 1), (1, 0)])


def ordered(axis, mine, other):
    first = lax.axis_index(axis) == 0
    return jnp.stack([jnp.where(first, mine, other), jnp.where(first, other, mine)])


def spread(value, axis):
    parts = [value] + [lax.ppermute(value, axis, [(i, i ^ k) for i in range(4)]) for k in (1, 2, 3)]
    me = lax.axis_index(axis)
    odd, high = me % 2 == 1, me >= 2
    parts = [jnp.where(odd, parts[s ^ 1], parts[s]) for s in range(4)]
    return jnp.stack([jnp.where(high, parts[s ^ 2], parts[s]) for s in range(4)])


def partial_kernel(zp_ref, all_ref, own_ref, low_ref, high_ref, out_ref, rows, bases, outs, sems):
    n, low = rows.shape[1], low_ref.shape[0]
    loads = [
        (own_ref, bases.at[0]),
        (all_ref.at[pl.ds(0, n)], rows.at[0]),
        (low_ref, bases.at[1, pl.ds(0, low)]),
        (high_ref, bases.at[1, pl.ds(low, high_ref.shape[0])]),
        (all_ref.at[pl.ds(n, n)], rows.at[1]),
    ]
    loads = [pltpu.make_async_copy(a, b, sems.at[i]) for i, (a, b) in enumerate(loads)]
    for load in loads:
        load.start()
    zp = zp_ref[0]
    stores = []
    for h, which, needed in ((0, 0, loads[:2]), (0, 1, loads[2:4]), (1, 0, loads[4:]), (1, 1, ())):
        for load in needed:
            load.wait()
        part = lax.dot_general(
            bases[which], rows[h], (((1,), (1,)), ((), ())), preferred_element_type=F32
        ).astype(BF16)
        at, width = len(stores), outs.shape[3]
        for i in range(4):
            outs[at, i] = part[:, i * width : (i + 1) * width]
        place = zp if which == 0 else 1 - zp
        stores.append(
            pltpu.make_async_copy(outs.at[at], out_ref.at[pl.ds(place * 8 + h * 4, 4)], sems.at[5 + at])
        )
        stores[-1].start()
    for store in stores:
        store.wait()


def partial_sums(gathered, own, other):
    rows, feats = gathered.shape[0] // 2, gathered.shape[1]
    outs = own.shape[0]
    whole = pl.BlockSpec(memory_space=pl.ANY)
    return pl.pallas_call(
        partial_kernel,
        out_shape=jax.ShapeDtypeStruct((16, outs, rows // 4), BF16),
        in_specs=[pl.BlockSpec(memory_space=pltpu.SMEM)] + [whole] * 4,
        out_specs=whole,
        scratch_shapes=[
            pltpu.VMEM((2, rows, feats), BF16),
            pltpu.VMEM((2, outs, feats), BF16),
            pltpu.VMEM((4, 4, outs, rows // 4), BF16),
            pltpu.SemaphoreType.DMA((9,)),
        ],
        compiler_params=pltpu.CompilerParams(vmem_limit_bytes=60 * 2**20),
        cost_estimate=pl.CostEstimate(
            flops=8 * rows * feats * outs, bytes_accessed=4 * rows * feats, transcendentals=0
        ),
    )(lax.axis_index("zp").reshape(1), gathered, own, *other)


def on_device(grads, acts, grad_basis, act_basis):
    half = grads.shape[0]
    quarter, feats = acts.shape[0] // 4, acts.shape[1]
    cols = act_basis.shape[1]
    own_basis = grad_basis.T

    other = swap(grads, "zq")
    act = lax.all_to_all(acts.reshape(4, quarter, feats), ("zq", "zp"), 0, 0)
    other, act = tie([other, act])
    gathered = lax.all_gather(jnp.concatenate([grads, other], 0), "y", axis=0, tiled=True)

    act = ordered("zh", act, swap(act, "zh"))
    cut = 256
    send, act, act_basis = tie([own_basis[:cut], act, act_basis])
    other_basis = [swap(send, "zp")]
    basis = spread(act_basis, ("zq", "zp"))
    act = spread(act, "x")
    send, act = tie([own_basis[cut:], act], other_basis)
    other_basis.append(swap(send, "zp"))
    act = ordered("core", act, swap(act, "core"))
    act = act.reshape(16, 4, quarter, feats)
    rot = sum(dot(act[:, s].reshape(-1, feats), basis[s]) for s in range(4))
    rot = rot.astype(BF16).reshape(2, 8, quarter, cols).transpose(1, 0, 2, 3)
    rot = lax.all_to_all(rot, "y", 0, 0)
    (rot,) = tie([rot], other_basis)
    rot = rot.astype(F32).sum(0)
    sq = spread((rot * rot).astype(BF16), ("zq", "zp"))
    sq = sq.reshape(2, 2, 2, quarter, cols)
    first = lax.axis_index("zq") == 0
    sq = jnp.stack([jnp.where(first, sq[:, :, 0], sq[:, :, 1]), jnp.where(first, sq[:, :, 1], sq[:, :, 0])], 1)
    sq = sq.reshape(-1, cols)
    sq_act = lax.all_gather(sq, "y", axis=0, tiled=True)

    part = partial_sums(gathered, own_basis, other_basis)
    part = lax.all_to_all(part, ("zp", "core", "x"), 0, 0)
    part = part.transpose(0, 2, 1).reshape(2, 8, 2 * half, -1).astype(F32).sum(1)
    rot = part + swap(part.astype(BF16), "zh").astype(F32)
    sq = lax.all_gather((rot * rot).astype(BF16), "x", axis=0)
    mine, there = (v.reshape(8, 2 * half, -1) for v in (sq, swap(sq, "core")))
    tokens = sq_act.shape[0] // 2
    core = lax.axis_index("core")
    total = sum(
        lax.dot_general(
            g,
            lax.dynamic_slice_in_dim(sq_act, at * tokens, tokens, 0).reshape(8, 2 * half, cols),
            (((0, 1), (0, 1)), ((), ())),
            preferred_element_type=F32,
        )
        for g, at in ((mine, core), (there, 1 - core))
    )
    return total / F32(2 * tokens)


def solution(mesh):
    return jax.shard_map(
        on_device,
        mesh=Mesh(mesh.devices.reshape(SPLIT), AXES),
        in_specs=(P(TOK, COL), P(COL, TOK), P(COL, TOK), P(TOK, COL)),
        out_specs=P(TOK, COL),
        check_vma=False,
    )
```

```python
import jax
import jax.numpy as jnp
from jax import lax
from jax.experimental import pallas as pl
from jax.experimental.pallas import tpu as pltpu
from jax.sharding import Mesh, PartitionSpec as P

F32, BF16 = jnp.float32, jnp.bfloat16
SPLIT = (8, 2, 2, 4, 2, 2)
AXES = ("y", "zq", "zp", "x", "zh", "core")
TOK, COL = ("y", "zq", "zp"), ("x", "zh", "core")


def dot(a, b):
    return jnp.dot(a, b, preferred_element_type=F32)


def tie(values, earlier=()):
    n = len(values)
    whole = pl.BlockSpec(memory_space=pl.ANY)
    return pl.pallas_call(
        lambda *refs: None,
        out_shape=[jax.ShapeDtypeStruct(v.shape, v.dtype) for v in values],
        in_specs=[whole] * (n + len(earlier)),
        out_specs=[whole] * n,
        input_output_aliases={i: i for i in range(n)},
    )(*values, *earlier)


def shift(value, axis, by):
    n = lax.axis_size(axis)
    return lax.ppermute(value, axis, [(i, (i + by) % n) for i in range(n)])


def swap(value, axis):
    return lax.ppermute(value, axis, [(0, 1), (1, 0)])


def ordered(axis, mine, other):
    first = lax.axis_index(axis) == 0
    return jnp.stack([jnp.where(first, mine, other), jnp.where(first, other, mine)])


def spread(value, axis):
    parts = [value] + [lax.ppermute(value, axis, [(i, i ^ k) for i in range(4)]) for k in (1, 2, 3)]
    me = lax.axis_index(axis)
    odd, high = me % 2 == 1, me >= 2
    parts = [jnp.where(odd, parts[s ^ 1], parts[s]) for s in range(4)]
    return jnp.stack([jnp.where(high, parts[s ^ 2], parts[s]) for s in range(4)])


def partial_kernel(zp_ref, all_ref, own_ref, low_ref, high_ref, out_ref, rows, bases, outs, sems):
    n, low = rows.shape[1], low_ref.shape[0]
    loads = [
        (own_ref, bases.at[0]),
        (all_ref.at[pl.ds(0, n)], rows.at[0]),
        (low_ref, bases.at[1, pl.ds(0, low)]),
        (high_ref, bases.at[1, pl.ds(low, high_ref.shape[0])]),
        (all_ref.at[pl.ds(n, n)], rows.at[1]),
    ]
    loads = [pltpu.make_async_copy(a, b, sems.at[i]) for i, (a, b) in enumerate(loads)]
    for load in loads:
        load.start()
    zp = zp_ref[0]
    stores = []
    for h, which, needed in ((0, 0, loads[:2]), (0, 1, loads[2:4]), (1, 0, loads[4:]), (1, 1, ())):
        for load in needed:
            load.wait()
        part = lax.dot_general(
            bases[which], rows[h], (((1,), (1,)), ((), ())), preferred_element_type=F32
        ).astype(BF16)
        at, width = len(stores), outs.shape[3]
        for i in range(4):
            outs[at, i] = part[:, i * width : (i + 1) * width]
        place = zp if which == 0 else 1 - zp
        stores.append(
            pltpu.make_async_copy(outs.at[at], out_ref.at[pl.ds(place * 8 + h * 4, 4)], sems.at[5 + at])
        )
        stores[-1].start()
    for store in stores:
        store.wait()


def partial_sums(gathered, own, other):
    rows, feats = gathered.shape[0] // 2, gathered.shape[1]
    outs = own.shape[0]
    whole = pl.BlockSpec(memory_space=pl.ANY)
    return pl.pallas_call(
        partial_kernel,
        out_shape=jax.ShapeDtypeStruct((16, outs, rows // 4), BF16),
        in_specs=[pl.BlockSpec(memory_space=pltpu.SMEM)] + [whole] * 4,
        out_specs=whole,
        scratch_shapes=[
            pltpu.VMEM((2, rows, feats), BF16),
            pltpu.VMEM((2, outs, feats), BF16),
            pltpu.VMEM((4, 4, outs, rows // 4), BF16),
            pltpu.SemaphoreType.DMA((9,)),
        ],
        compiler_params=pltpu.CompilerParams(vmem_limit_bytes=60 * 2**20),
        cost_estimate=pl.CostEstimate(
            flops=8 * rows * feats * outs, bytes_accessed=4 * rows * feats, transcendentals=0
        ),
    )(lax.axis_index("zp").reshape(1), gathered, own, *other)


def on_device(grads, acts, grad_basis, act_basis):
    half = grads.shape[0]
    quarter, feats = acts.shape[0] // 4, acts.shape[1]
    cols = act_basis.shape[1]
    own_basis = grad_basis.T

    other = swap(grads, "zq")
    act = lax.all_to_all(acts.reshape(4, quarter, feats), ("zq", "zp"), 0, 0)
    other, act = tie([other, act])
    gathered = lax.all_gather(jnp.concatenate([grads, other], 0), "y", axis=0, tiled=True)

    act = ordered("zh", act, swap(act, "zh"))
    cut = 256
    send, act, act_basis = tie([own_basis[:cut], act, act_basis])
    other_basis = [swap(send, "zp")]
    basis = spread(act_basis, ("zq", "zp"))
    act = spread(act, "x")
    send, act, basis = tie([own_basis[cut:], act, basis], other_basis)
    other_basis.append(swap(send, "zp"))
    act = ordered("core", act, swap(act, "core"))
    act = act.reshape(16, 4, quarter, feats)
    rot = sum(dot(act[:, s].reshape(-1, feats), basis[s]) for s in range(4))
    rot = rot.astype(BF16).reshape(2, 8, quarter, cols).transpose(1, 0, 2, 3)
    rot = lax.all_to_all(rot, "y", 0, 0)
    (rot,) = tie([rot], other_basis)
    rot = rot.astype(F32).sum(0)
    sq = spread((rot * rot).astype(BF16), ("zq", "zp"))
    sq = sq.reshape(2, 2, 2, quarter, cols)
    first = lax.axis_index("zq") == 0
    sq = jnp.stack([jnp.where(first, sq[:, :, 0], sq[:, :, 1]), jnp.where(first, sq[:, :, 1], sq[:, :, 0])], 1)
    sq = sq.reshape(-1, cols)
    sq_act = lax.all_gather(sq, "y", axis=0, tiled=True)

    part = partial_sums(gathered, own_basis, other_basis)
    part = lax.all_to_all(part, ("zp", "core", "x"), 0, 0)
    part = part.transpose(0, 2, 1).reshape(2, 8, 2 * half, -1).astype(F32).sum(1)
    rot = part + swap(part.astype(BF16), "zh").astype(F32)
    sq = lax.all_gather((rot * rot).astype(BF16), "x", axis=0)
    mine, there = (v.reshape(8, 2 * half, -1) for v in (sq, swap(sq, "core")))
    tokens = sq_act.shape[0] // 2
    core = lax.axis_index("core")
    total = sum(
        lax.dot_general(
            g,
            lax.dynamic_slice_in_dim(sq_act, at * tokens, tokens, 0).reshape(8, 2 * half, cols),
            (((0, 1), (0, 1)), ((), ())),
            preferred_element_type=F32,
        )
        for g, at in ((mine, core), (there, 1 - core))
    )
    return total / F32(2 * tokens)


def solution(mesh):
    return jax.shard_map(
        on_device,
        mesh=Mesh(mesh.devices.reshape(SPLIT), AXES),
        in_specs=(P(TOK, COL), P(COL, TOK), P(COL, TOK), P(TOK, COL)),
        out_specs=P(TOK, COL),
        check_vma=False,
    )
```
